32 devices in a mesh: gx: 4 (over y, x), gy: 4 (over z), gz: 2 (over core).
Axes of the slice: x: 2, y: 2, z: 4, core: 2. Of those that a mesh axis runs over, the one named last changes fastest.
Arguments:
- displacement: bfloat16 [4, 4, 2, 768, 128], P('gx', 'gy', 'gz'), may hold values from -6 to 6
- flexibility: bfloat16 [4, 4, 2, 768, 768], P('gx', 'gy', 'gz'), as said below
- schur: bfloat16 [4, 4, 2, 768, 768], P('gx', 'gy', 'gz'), as said below
- face_rows: int32 [4, 4, 2, 768], P('gx', 'gy', 'gz'), may hold values from 0 to 767, as said below
- multiplicity: int32 [4, 4, 2, 768], P('gx', 'gy', 'gz'), may hold values from 2 to 8, as said below
Outputs:
- multipliers: float32 [4, 4, 2, 768, 128], P('gx', 'gy', 'gz')
The draws below stay inside these ranges and needn't reach their ends.
Inputs may be any that keep to these rules, and one draw needn't show every extreme that they name: `flexibility`: symmetric and positive definite. `schur`: symmetric and positive definite. `face_rows`: an interface unknown may be constrained by several slots of its subdomain. `multiplicity`: each value is 2, 4 or 8; a slot and its partner slot carry the same value.
All inputs are finite; a program needn't handle non-finite values.
Results may differ from the reference program's by a relative error of at most 0.017.
Values may be sent and summed in bfloat16 or wider, within the bound.
A program may use at most 64 MiB of HBM per device.

```python
import jax
import jax.numpy as jnp
from jax import lax

NI = 768
FACE = 128
LOADS = 128
ITERS = 3
NS = 768
N_GX = 4
N_GY = 4
N_GZ = 2


def sym_operator(key, low, high):
    key_a, key_b = jax.random.split(key)
    shape = (N_GX, N_GY, N_GZ, NI, NI)
    noise = jax.random.normal(key_a, shape, jnp.float32) * (1.0 / (2.0 * NI)) ** 0.5
    diagonal = jax.random.uniform(key_b, (N_GX, N_GY, N_GZ, NI), jnp.float32, low, high)
    sym = (noise + jnp.swapaxes(noise, -1, -2)) * 0.7071067811865476
    return sym + diagonal[..., None] * jnp.eye(NI, dtype=jnp.float32)


def draw_flexibility(key, part):
    return sym_operator(jax.random.fold_in(key, 11), 3.0, 6.0).astype(jnp.bfloat16)


def draw_schur(key, part):
    return sym_operator(jax.random.fold_in(key, 23), 2.5, 5.0).astype(jnp.bfloat16)


def draw_face_rows(key, part):
    count = N_GX * N_GY * N_GZ
    keys = jax.random.split(jax.random.fold_in(key, 37), count)

    def one_list(sub):
        key_p, key_s, key_d = jax.random.split(sub, 3)
        order = jax.random.permutation(key_p, NI).astype(jnp.int32)
        base = jnp.take(order, jnp.arange(NS, dtype=jnp.int32) % NI)
        number = NS // 8
        source = jax.random.randint(key_s, (number,), 0, NS, dtype=jnp.int32)
        target = jax.random.randint(key_d, (number,), 0, NS, dtype=jnp.int32)
        return base.at[target].set(base[source])
    return jax.vmap(one_list)(keys).reshape(N_GX, N_GY, N_GZ, NS).astype(jnp.int32)


def draw_multiplicity(key, part):
    levels = jax.random.randint(jax.random.fold_in(key, 53), (N_GX, N_GY, N_GZ, 6, FACE), 1, 4, dtype=jnp.int32)
    values = jnp.where(levels == 1, 2, jnp.where(levels == 2, 4, 8)).astype(jnp.int32)
    coord_x = jnp.arange(N_GX).reshape(N_GX, 1, 1, 1)
    coord_y = jnp.arange(N_GY).reshape(1, N_GY, 1, 1)
    coord_z = jnp.arange(N_GZ).reshape(1, 1, N_GZ, 1)
    face_a = jnp.where(coord_x > 0, jnp.roll(values[:, :, :, 1], 1, axis=0), values[:, :, :, 0])
    face_c = jnp.where(coord_y > 0, jnp.roll(values[:, :, :, 3], 1, axis=1), values[:, :, :, 2])
    face_e = jnp.where(coord_z > 0, jnp.roll(values[:, :, :, 5], 1, axis=2), values[:, :, :, 4])
    joined = jnp.stack([face_a, values[:, :, :, 1], face_c, values[:, :, :, 3], face_e, values[:, :, :, 5]], axis=3)
    return joined.reshape(N_GX, N_GY, N_GZ, NS).astype(jnp.int32)


def level_of(rng, shape, shards, low, high):
    def one(position, blocks):
        heights = jax.random.uniform(jax.random.fold_in(jax.random.fold_in(rng, 6), position), (blocks,), jnp.float32, low / len(shards), high / len(shards))
        return jnp.repeat(jnp.exp(heights), shape[position] // blocks).reshape((-1,) + (1,) * (len(shape) - position - 1))

    level = one(*shards[0])
    for cut in shards[1:]:
        level = level * one(*cut)
    return level


def scatter_about(stream_key, extent, deviation, reach, pieces=(), kind=jnp.bfloat16):
    gain = level_of(stream_key, extent, pieces, -0.22, 0.18) if pieces else 1.0
    entries = jax.random.normal(stream_key, extent, jnp.float32) * deviation * gain
    return jnp.minimum(jnp.maximum(entries, -reach), reach).astype(kind)


def setup_inputs(seed: int = 0) -> dict:
    arg_keys = jax.random.split(jax.random.key(seed), 6)
    displacement = scatter_about(arg_keys[0], (N_GX, N_GY, N_GZ, NI, LOADS), 1.0, 6.0, ((0, 4), (1, 4), (2, 2)))
    flexibility = draw_flexibility(jax.random.fold_in(arg_keys[5], 71), 0)
    schur = draw_schur(jax.random.fold_in(arg_keys[5], 71), 0)
    face_rows = draw_face_rows(jax.random.fold_in(arg_keys[5], 71), 0)
    multiplicity = draw_multiplicity(jax.random.fold_in(arg_keys[5], 71), 0)
    return dict(displacement=displacement, flexibility=flexibility, schur=schur, face_rows=face_rows, multiplicity=multiplicity)


def shift_from(values, axis, lower):
    size = values.shape[axis]
    widths = [(0, 0)] * values.ndim
    widths[axis] = (1, 1)
    padded = jnp.pad(values, widths)
    start = 0 if lower else 2
    return lax.slice_in_dim(padded, start, start + size, axis=axis)


def reference(displacement, flexibility, schur, face_rows, multiplicity):
    count = N_GX * N_GY * N_GZ
    displaced = displacement.reshape(count, NI, LOADS)
    flex_ops = flexibility.reshape(count, NI, NI)
    schur_ops = schur.reshape(count, NI, NI)
    row_list = face_rows.reshape(count, NS)
    weight = 2.0 / multiplicity.reshape(count, NS, 1).astype(jnp.float32)
    shape3 = (N_GX, N_GY, N_GZ)
    coord_x = jnp.broadcast_to(jnp.arange(N_GX).reshape(N_GX, 1, 1), shape3)
    coord_y = jnp.broadcast_to(jnp.arange(N_GY).reshape(1, N_GY, 1), shape3)
    coord_z = jnp.broadcast_to(jnp.arange(N_GZ).reshape(1, 1, N_GZ), shape3)
    have = jnp.stack([coord_x > 0, coord_x < N_GX - 1, coord_y > 0, coord_y < N_GY - 1, coord_z > 0, coord_z < N_GZ - 1], axis=-1)
    inner = jnp.where(have, 0.5, 1.0).astype(jnp.float32)
    inner = jnp.repeat(inner[..., None], FACE, axis=-1).reshape(count, NS, 1)

    def pick(values):
        return jax.vmap(lambda block, picks: jnp.take(block, picks, axis=0))(values, row_list)

    def jump(values):
        faces_all = pick(values).astype(jnp.float32).reshape(N_GX, N_GY, N_GZ, 6, FACE, LOADS)
        partner = jnp.stack([
            shift_from(faces_all[:, :, :, 1], 0, True),
            shift_from(faces_all[:, :, :, 0], 0, False),
            shift_from(faces_all[:, :, :, 3], 1, True),
            shift_from(faces_all[:, :, :, 2], 1, False),
            shift_from(faces_all[:, :, :, 5], 2, True),
            shift_from(faces_all[:, :, :, 4], 2, False)], axis=3)
        return (faces_all - partner).reshape(count, NS, LOADS)

    def spread(values):
        summed = jax.vmap(lambda block, picks: jnp.zeros((NI, LOADS), jnp.float32).at[picks].add(block))(values, row_list)
        return summed.astype(jnp.bfloat16)

    def product(operators, vectors):
        return lax.map(lambda pair: jnp.dot(pair[0], pair[1], preferred_element_type=jnp.float32).astype(jnp.bfloat16), (operators, vectors))

    def flex_apply(values):
        return jump(product(flex_ops, spread(values)))

    def precondition(values):
        return weight * jump(product(schur_ops, spread(weight * values)))

    def inner_product(left, right):
        return jnp.sum(inner * left * right, axis=(0, 1))

    residual = jump(displaced)
    solution = jnp.zeros((count, NS, LOADS), jnp.float32)
    smoothed = precondition(residual)
    direction = smoothed
    rho_now = inner_product(residual, smoothed)
    for iteration in range(ITERS):
        image = flex_apply(direction)
        step_len = rho_now / inner_product(direction, image)
        solution = solution + step_len * direction
        residual = residual - step_len * image
        if iteration + 1 < ITERS:
            smoothed = precondition(residual)
            rho_next = inner_product(residual, smoothed)
            direction = smoothed + (rho_next / rho_now) * direction
            rho_now = rho_next
    return solution.reshape(N_GX, N_GY, N_GZ, NS, LOADS)
```

```python
import functools

import jax
import jax.numpy as jnp
from jax import lax
from jax.experimental import pallas as pl
from jax.experimental.pallas import tpu as pltpu
from jax.sharding import PartitionSpec as P

ITERS = 3
AXES = ("gx", "gy", "gz")
STAGES = ("gz", "gy", "gx")
MESH = pl.DeviceIdType.MESH
F32 = jnp.float32
BF16 = jnp.bfloat16


def dot(a, b):
    return jnp.dot(a, b, preferred_element_type=F32)


def kernel(sizes, disp, flex, schur, rows, mult, out, table, picks, wpicks, temp,
           op_a, op_b, send, recv, res, smo, img, along, across, way, vec, red_out, red_in,
           send_sem, recv_sem, red_send_sem, red_recv_sem):
    width, loads = disp.shape
    faces, length = rows.shape
    slots = faces * length
    index = {a: lax.axis_index(a) for a in AXES}
    barrier = pltpu.get_barrier_semaphore()
    peers = 0
    for a in AXES:
        for d in range(1, sizes[a]):
            pl.semaphore_signal(barrier, inc=1, device_id={a: lax.rem(index[a] + d, sizes[a])},
                                device_id_type=MESH)
            peers += 1

    have, toward = [], []
    for a in AXES:
        have += [index[a] > 0, index[a] < sizes[a] - 1]
        toward += [{a: lax.rem(index[a] + sizes[a] - 1, sizes[a])},
                   {a: lax.rem(index[a] + 1, sizes[a])}]
    half = [jnp.where(h, 0.5, 1.0).astype(F32) for h in have]

    def block(f):
        return slice(f * length, (f + 1) * length)

    exchanges = send.shape[0]
    for f in range(faces):
        @pl.when(jnp.logical_not(have[f]))
        def _():
            for e in range(exchanges):
                recv[e, f] = jnp.zeros((length, loads), BF16)

    def face_copy(e, f):
        return pltpu.make_async_remote_copy(
            src_ref=send.at[e, f], dst_ref=recv.at[e, f ^ 1], send_sem=send_sem.at[e, f],
            recv_sem=recv_sem.at[e, f ^ 1], device_id=toward[f], device_id_type=MESH)

    def face_arrival(e, f):
        return pltpu.make_async_remote_copy(
            src_ref=send.at[e, f], dst_ref=recv.at[e, f], send_sem=send_sem.at[e, f],
            recv_sem=recv_sem.at[e, f], device_id=toward[f], device_id_type=MESH)

    def post(e, f, value):
        send[e, f] = value.astype(BF16)

        @pl.when(have[f])
        def _():
            face_copy(e, f).start()

    def jumped(e, f):
        @pl.when(have[f])
        def _():
            face_arrival(e, f).wait_recv()
        return send[e, f].astype(F32) - recv[e, f].astype(F32)

    def red_copy(k, s, d):
        a = STAGES[s]
        return pltpu.make_async_remote_copy(
            src_ref=red_out.at[k, s], dst_ref=red_in.at[k, s, d - 1],
            send_sem=red_send_sem.at[k, s, d - 1], recv_sem=red_recv_sem.at[k, s, d - 1],
            device_id={a: lax.rem(index[a] + d, sizes[a])}, device_id_type=MESH)

    def red_start(k, s, value):
        red_out[k, s] = value
        for d in range(1, sizes[STAGES[s]]):
            red_copy(k, s, d).start()

    def red_finish(k, s):
        total = red_out[k, s]
        for d in range(1, sizes[STAGES[s]]):
            red_copy(k, s, d).wait_recv()
            total = total + red_in[k, s, d - 1]
        return total

    def pair(first, second):
        line = lax.broadcasted_iota(jnp.int32, (8, loads), 0)
        return jnp.where(line == 0, first, jnp.where(line == 1, second, 0.0))

    def total_of(value):
        return jnp.sum(value, axis=0, keepdims=True)

    lanes = lax.broadcasted_iota(jnp.int32, (length, length), 1)
    lines = lax.broadcasted_iota(jnp.int32, (length, length), 0)
    for f in range(faces):
        row = jnp.broadcast_to(rows[f:f + 1, :], (length, length))
        weight = jnp.broadcast_to(2.0 / mult[f:f + 1, :].astype(F32), (length, length))
        row_t = row.astype(F32).T.astype(jnp.int32)
        weight_t = weight.T
        for c in range(width // length):
            table[block(c), block(f)] = jnp.where(row == lines + c * length, 1.0, 0.0).astype(BF16)
            hit = row_t == lanes + c * length
            picks[block(f), block(c)] = jnp.where(hit, 1.0, 0.0).astype(BF16)
            wpicks[block(f), block(c)] = jnp.where(hit, weight_t, 0.0).astype(BF16)

    pl.semaphore_wait(barrier, peers)
    moved = disp[...]
    for f in range(faces):
        post(0, f, dot(picks[block(f), :], moved))

    def gather(left, op, scale, result):
        @pl.loop(0, width // length)
        def _(i):
            part = pl.ds(pl.multiple_of(i * length, length), length)
            temp[part, :] = dot(op[part, :], table[...]).astype(BF16)

        @pl.loop(0, faces)
        def _(i):
            part = pl.ds(pl.multiple_of(i * length, length), length)
            value = dot(left[part, :], temp[...])
            if scale is not None:
                value = value * scale
            result[part, :] = value.astype(BF16)

    weight_row = jnp.concatenate([2.0 / mult[f:f + 1, :].astype(F32) for f in range(faces)], axis=1)
    gather(wpicks, schur, weight_row, op_b)

    for f in range(faces):
        value = jumped(0, f)
        res[block(f), :] = value
        vec[block(f), :] = value.astype(BF16)
    x = vec[...]
    for f in range(faces):
        post(1, f, dot(op_b[block(f), :], x))
    gather(picks, flex, None, op_a)
    rho = jnp.zeros((1, loads), F32)
    for f in range(faces):
        value = jumped(1, f)
        smo[block(f), :] = value
        vec[block(f), :] = value.astype(BF16)
        rho = rho + half[f] * total_of(res[block(f), :] * value)

    alpha = rho_old = None
    for k in range(ITERS):
        last = k + 1 == ITERS
        e = 2 + 2 * k
        x = vec[...]
        curve = jnp.zeros((1, loads), F32)
        for f in range(faces):
            y = dot(op_a[block(f), :], x)
            if not last:
                post(e, f, y)
            curve = curve + total_of(smo[block(f), :] * y)
        red_start(k, 0, pair(rho, curve))
        if last:
            red_start(k, 1, red_finish(k, 0))
            red_start(k, 2, red_finish(k, 1))
        else:
            for f in range(faces):
                value = jumped(e, f)
                img[block(f), :] = value
                vec[block(f), :] = value.astype(BF16)
            red_start(k, 1, red_finish(k, 0))
            x = vec[...]
            for f in range(faces):
                post(e + 1, f, dot(op_b[block(f), :], x))
            red_start(k, 2, red_finish(k, 1))
        sums = red_finish(k, 2)
        rho_now, curve = sums[0:1, :], sums[1:2, :]
        if k == 0:
            beta = None
            alpha = rho_now / curve
        else:
            beta = rho_now / rho_old
            alpha = rho_now / (curve - beta * rho_now / alpha)
        rho_old = rho_now
        rho = jnp.zeros((1, loads), F32)
        for f in range(faces):
            b = block(f)
            p = smo[b, :] if beta is None else smo[b, :] + beta * way[b, :]
            total = alpha * p if beta is None else out[b, :] + alpha * p
            out[b, :] = total
            if last:
                continue
            way[b, :] = p
            q = jumped(e + 1, f)
            s = img[b, :]
            if beta is not None:
                q = q + beta * across[b, :]
                s = s + beta * along[b, :]
            across[b, :] = q
            along[b, :] = s
            r = res[b, :] - alpha * s
            z = smo[b, :] - alpha * q
            res[b, :] = r
            smo[b, :] = z
            vec[b, :] = z.astype(BF16)
            rho = rho + half[f] * total_of(r * z)

    for f in range(faces):
        @pl.when(have[f])
        def _():
            for e in range(exchanges):
                face_copy(e, f).wait_send()
    for k in range(ITERS):
        for s in range(len(STAGES)):
            for d in range(1, sizes[STAGES[s]]):
                red_copy(k, s, d).wait_send()


def shards(sizes, displacement, flexibility, schur, face_rows, multiplicity):
    width = flexibility.shape[-1]
    loads = displacement.shape[-1]
    slots = face_rows.shape[-1]
    length = slots // 6
    exchanges = 2 * ITERS
    most = max(max(sizes.values()) - 1, 1)
    vmem = pl.BlockSpec(memory_space=pltpu.VMEM)
    state = pltpu.VMEM((slots, loads), F32)
    result = pl.pallas_call(
        functools.partial(kernel, sizes),
        out_shape=jax.ShapeDtypeStruct((slots, loads), F32),
        in_specs=[vmem] * 5,
        out_specs=vmem,
        scratch_shapes=[
            pltpu.VMEM((width, slots), BF16),
            pltpu.VMEM((slots, width), BF16),
            pltpu.VMEM((slots, width), BF16),
            pltpu.VMEM((width, slots), BF16),
            pltpu.VMEM((slots, slots), BF16),
            pltpu.VMEM((slots, slots), BF16),
            pltpu.VMEM((exchanges, 6, length, loads), BF16),
            pltpu.VMEM((exchanges, 6, length, loads), BF16),
            state, state, state, state, state, state,
            pltpu.VMEM((slots, loads), BF16),
            pltpu.VMEM((ITERS, 3, 8, loads), F32),
            pltpu.VMEM((ITERS, 3, most, 8, loads), F32),
            pltpu.SemaphoreType.DMA((exchanges, 6)),
            pltpu.SemaphoreType.DMA((exchanges, 6)),
            pltpu.SemaphoreType.DMA((ITERS, 3, most)),
            pltpu.SemaphoreType.DMA((ITERS, 3, most)),
        ],
        compiler_params=pltpu.CompilerParams(
            collective_id=0, has_side_effects=True, vmem_limit_bytes=44 * 1024 * 1024),
    )(
        displacement.reshape(width, loads),
        flexibility.reshape(width, width),
        schur.reshape(width, width),
        face_rows.reshape(6, length),
        multiplicity.reshape(6, length),
    )
    return result.reshape(1, 1, 1, slots, loads)


def solution(mesh):
    whole = P(*AXES, None, None)
    lists = P(*AXES, None)
    return jax.shard_map(
        functools.partial(shards, {a: mesh.shape[a] for a in AXES}),
        mesh=mesh,
        in_specs=(whole, whole, whole, lists, lists),
        out_specs=whole,
        check_vma=False,
    )
```

```python
import functools
import math

import jax
import jax.numpy as jnp
from jax import lax
from jax.experimental import pallas as pl
from jax.experimental.pallas import tpu as pltpu
from jax.sharding import PartitionSpec as P

ITERS = 3
AXES = ("gx", "gy", "gz")
STAGES = (("gz",), ("gx", "gy"))
GROUP = 2
MESH = pl.DeviceIdType.MESH
F32 = jnp.float32
BF16 = jnp.bfloat16


def dot(a, b):
    return jnp.dot(a, b, preferred_element_type=F32)


def kernel(sizes, disp_in, flex_in, schur_in, rows, mult, out_ref, disp, flex, schur, table, picks, wpicks, temp,
           op_a, op_b, send, recv, res, smo, img, along, across, way, vec, red_out, red_in,
           load_sem, send_sem, recv_sem, red_send_sem, red_recv_sem):
    loads_in = [pltpu.make_async_copy(a.at[0, 0, 0], b, load_sem.at[i])
                for i, (a, b) in enumerate(((disp_in, disp), (schur_in, schur), (flex_in, flex)))]
    for copy in loads_in:
        copy.start()
    width, loads = disp.shape
    slots = rows.shape[-1]
    faces = 6
    length = slots // faces
    out = out_ref.at[0, 0, 0]
    index = {a: lax.axis_index(a) for a in AXES}
    barrier = pltpu.get_barrier_semaphore()

    def count(s):
        return math.prod(sizes[a] for a in STAGES[s])

    def peer(s, d):
        if len(STAGES[s]) == 1:
            a = STAGES[s][0]
            return {a: lax.rem(index[a] + d, sizes[a])}
        a, b = STAGES[s]
        place = lax.rem(index[a] * sizes[b] + index[b] + d, count(s))
        return {a: place // sizes[b], b: lax.rem(place, sizes[b])}

    peers = 0
    for s in range(len(STAGES)):
        for d in range(1, count(s)):
            pl.semaphore_signal(barrier, inc=1, device_id=peer(s, d), device_id_type=MESH)
            peers += 1

    have, toward = [], []
    for a in AXES:
        have += [index[a] > 0, index[a] < sizes[a] - 1]
        toward += [{a: lax.rem(index[a] + sizes[a] - 1, sizes[a])},
                   {a: lax.rem(index[a] + 1, sizes[a])}]
    half = [jnp.where(h, 0.5, 1.0).astype(F32) for h in have]

    def block(f):
        return slice(f * length, (f + 1) * length)

    exchanges = send.shape[0]
    for f in range(faces):
        @pl.when(jnp.logical_not(have[f]))
        def _():
            for e in range(exchanges):
                recv[e, f] = jnp.zeros((length, loads), BF16)

    def face_copy(e, f):
        return pltpu.make_async_remote_copy(
            src_ref=send.at[e, f], dst_ref=recv.at[e, f ^ 1], send_sem=send_sem.at[e, f],
            recv_sem=recv_sem.at[e, f ^ 1], device_id=toward[f], device_id_type=MESH)

    def face_arrival(e, f):
        return pltpu.make_async_remote_copy(
            src_ref=send.at[e, f], dst_ref=recv.at[e, f], send_sem=send_sem.at[e, f],
            recv_sem=recv_sem.at[e, f], device_id=toward[f], device_id_type=MESH)

    def post(e, f, value):
        send[e, f] = value.astype(BF16)

        @pl.when(have[f])
        def _():
            face_copy(e, f).start()

    def jumped(e, f):
        @pl.when(have[f])
        def _():
            face_arrival(e, f).wait_recv()
        return send[e, f].astype(F32) - recv[e, f].astype(F32)

    def apply(op, vector, take):
        x = vector[...]
        for g in range(0, faces, GROUP):
            y = dot(op[g * length:(g + GROUP) * length, :], x)
            for f in range(g, g + GROUP):
                take(f, y[block(f - g), :])

    def red_copy(k, s, d):
        return pltpu.make_async_remote_copy(
            src_ref=red_out.at[k, s], dst_ref=red_in.at[k, s, d - 1],
            send_sem=red_send_sem.at[k, s, d - 1], recv_sem=red_recv_sem.at[k, s, d - 1],
            device_id=peer(s, d), device_id_type=MESH)

    def red_start(k, s, value):
        red_out[k, s] = value
        for d in range(1, count(s)):
            red_copy(k, s, d).start()

    def red_finish(k, s):
        total = red_out[k, s]
        for d in range(1, count(s)):
            red_copy(k, s, d).wait_recv()
            total = total + red_in[k, s, d - 1]
        return total

    def pair(first, second):
        line = lax.broadcasted_iota(jnp.int32, (8, loads), 0)
        return jnp.where(line == 0, first, jnp.where(line == 1, second, 0.0))

    def total_of(value):
        return jnp.sum(value, axis=0, keepdims=True)

    lanes = lax.broadcasted_iota(jnp.int32, (length, length), 1)
    lines = lax.broadcasted_iota(jnp.int32, (length, length), 0)
    for f in range(faces):
        row = jnp.broadcast_to(rows[0, 0, :, block(f)], (length, length))
        weight = jnp.broadcast_to(2.0 / mult[0, 0, :, block(f)].astype(F32), (length, length))
        row_t = row.astype(F32).T.astype(jnp.int32)
        weight_t = weight.T
        for c in range(width // length):
            table[block(c), block(f)] = jnp.where(row == lines + c * length, 1.0, 0.0).astype(BF16)
            hit = row_t == lanes + c * length
            picks[block(f), block(c)] = jnp.where(hit, 1.0, 0.0).astype(BF16)
            wpicks[block(f), block(c)] = jnp.where(hit, weight_t, 0.0).astype(BF16)

    pl.semaphore_wait(barrier, peers)
    loads_in[0].wait()
    apply(picks, disp, lambda f, y: post(0, f, y))

    def gather(left, op, scale, result):
        for i in range(faces // 2):
            part = slice(2 * i * length, 2 * (i + 1) * length)
            temp[:, part] = dot(op[...], table[:, part]).astype(BF16)
        for i in range(faces // 2):
            part = slice(2 * i * length, 2 * (i + 1) * length)
            value = dot(left[...], temp[:, part])
            if scale is not None:
                value = value * scale[:, part]
            result[:, part] = value.astype(BF16)

    weight_row = 2.0 / mult[0, 0].astype(F32)
    loads_in[1].wait()
    gather(wpicks, schur, weight_row, op_b)

    for f in range(faces):
        value = jumped(0, f)
        res[block(f), :] = value
        vec[block(f), :] = value.astype(BF16)
    apply(op_b, vec, lambda f, y: post(1, f, y))
    loads_in[2].wait()
    gather(picks, flex, None, op_a)
    rho = jnp.zeros((1, loads), F32)
    for f in range(faces):
        value = jumped(1, f)
        smo[block(f), :] = value
        vec[block(f), :] = value.astype(BF16)
        rho = rho + half[f] * total_of(res[block(f), :] * value)

    alpha = rho_old = None
    for k in range(ITERS):
        last = k + 1 == ITERS
        e = 2 + 2 * k
        parts = []

        def energy(f, y):
            if not last:
                post(e, f, y)
            parts.append(total_of(smo[block(f), :] * y))

        apply(op_a, vec, energy)
        red_start(k, 0, pair(rho, sum(parts)))
        if last:
            red_start(k, 1, red_finish(k, 0))
        else:
            for f in range(faces):
                value = jumped(e, f)
                img[block(f), :] = value
                vec[block(f), :] = value.astype(BF16)
            red_start(k, 1, red_finish(k, 0))
            apply(op_b, vec, lambda f, y: post(e + 1, f, y))
        sums = red_finish(k, 1)
        rho_now, curve = sums[0:1, :], sums[1:2, :]
        if k == 0:
            beta = None
            alpha = rho_now / curve
        else:
            beta = rho_now / rho_old
            alpha = rho_now / (curve - beta * rho_now / alpha)
        rho_old = rho_now
        rho = jnp.zeros((1, loads), F32)
        for f in range(faces):
            b = block(f)
            p = smo[b, :] if beta is None else smo[b, :] + beta * way[b, :]
            total = alpha * p if beta is None else out[b, :] + alpha * p
            out[b, :] = total
            if last:
                continue
            way[b, :] = p
            q = jumped(e + 1, f)
            s = img[b, :]
            if beta is not None:
                q = q + beta * across[b, :]
                s = s + beta * along[b, :]
            across[b, :] = q
            along[b, :] = s
            r = res[b, :] - alpha * s
            z = smo[b, :] - alpha * q
            res[b, :] = r
            smo[b, :] = z
            vec[b, :] = z.astype(BF16)
            rho = rho + half[f] * total_of(r * z)

    for f in range(faces):
        @pl.when(have[f])
        def _():
            for e in range(exchanges):
                face_copy(e, f).wait_send()
    for k in range(ITERS):
        for s in range(len(STAGES)):
            for d in range(1, count(s)):
                red_copy(k, s, d).wait_send()


def shards(sizes, displacement, flexibility, schur, face_rows, multiplicity):
    width = flexibility.shape[-1]
    loads = displacement.shape[-1]
    slots = face_rows.shape[-1]
    length = slots // 6
    exchanges = 2 * ITERS
    most = max(math.prod(sizes[a] for a in names) for names in STAGES)
    stages = len(STAGES)
    vmem = pl.BlockSpec(memory_space=pltpu.VMEM)
    state = pltpu.VMEM((slots, loads), F32)
    result = pl.pallas_call(
        functools.partial(kernel, sizes),
        out_shape=jax.ShapeDtypeStruct((1, 1, 1, slots, loads), F32),
        in_specs=[pl.BlockSpec(memory_space=pltpu.HBM)] * 3 + [vmem] * 2,
        out_specs=vmem,
        scratch_shapes=[
            pltpu.VMEM((width, loads), BF16),
            pltpu.VMEM((width, width), BF16),
            pltpu.VMEM((width, width), BF16),
            pltpu.VMEM((width, slots), BF16),
            pltpu.VMEM((slots, width), BF16),
            pltpu.VMEM((slots, width), BF16),
            pltpu.VMEM((width, slots), BF16),
            pltpu.VMEM((slots, slots), BF16),
            pltpu.VMEM((slots, slots), BF16),
            pltpu.VMEM((exchanges, 6, length, loads), BF16),
            pltpu.VMEM((exchanges, 6, length, loads), BF16),
            state, state, state, state, state, state,
            pltpu.VMEM((slots, loads), BF16),
            pltpu.VMEM((ITERS, stages, 8, loads), F32),
            pltpu.VMEM((ITERS, stages, most, 8, loads), F32),
            pltpu.SemaphoreType.DMA((3,)),
            pltpu.SemaphoreType.DMA((exchanges, 6)),
            pltpu.SemaphoreType.DMA((exchanges, 6)),
            pltpu.SemaphoreType.DMA((ITERS, stages, most)),
            pltpu.SemaphoreType.DMA((ITERS, stages, most)),
        ],
        compiler_params=pltpu.CompilerParams(
            collective_id=0, has_side_effects=True, vmem_limit_bytes=44 * 1024 * 1024),
    )(
        displacement, flexibility, schur,
        face_rows.reshape(1, 1, 1, slots), multiplicity.reshape(1, 1, 1, slots),
    )
    return result


def solution(mesh):
    whole = P(*AXES, None, None)
    lists = P(*AXES, None)
    return jax.shard_map(
        functools.partial(shards, {a: mesh.shape[a] for a in AXES}),
        mesh=mesh,
        in_specs=(whole, whole, whole, lists, lists),
        out_specs=whole,
        check_vma=False,
    )
```

```python
import functools
import math

import jax
import jax.numpy as jnp
from jax import lax
from jax.experimental import pallas as pl
from jax.experimental.pallas import tpu as pltpu
from jax.sharding import PartitionSpec as P

ITERS = 3
AXES = ("gx", "gy", "gz")
STAGES = (("gz",), ("gx", "gy"))
GROUP = 2
ARRIVE = (4, 5, 2, 3, 0, 1)
MESH = pl.DeviceIdType.MESH
F32 = jnp.float32
BF16 = jnp.bfloat16


def dot(a, b):
    return jnp.dot(a, b, preferred_element_type=F32)


def kernel(sizes, disp_in, flex_in, schur_in, rows_in, mult_in, out_ref, disp, flex, schur,
           rows, mult, table, picks, wpicks, temp,
           op_a, op_b, send, recv, res, smo, img, along, across, way, vec, red_out, red_in,
           load_sem, send_sem, recv_sem, red_send_sem, red_recv_sem):
    lists_in = [pltpu.make_async_copy(rows_in, rows, load_sem.at[3]),
                pltpu.make_async_copy(mult_in, mult, load_sem.at[4])]
    loads_in = [pltpu.make_async_copy(a.at[0, 0, 0], b, load_sem.at[i])
                for i, (a, b) in enumerate(((disp_in, disp), (schur_in, schur), (flex_in, flex)))]
    for copy in lists_in + loads_in:
        copy.start()
    width, loads = disp.shape
    slots = rows.shape[-1]
    faces = 6
    length = slots // faces
    out = out_ref.at[0, 0, 0]
    index = {a: lax.axis_index(a) for a in AXES}
    barrier = pltpu.get_barrier_semaphore()

    def count(s):
        return math.prod(sizes[a] for a in STAGES[s])

    def peer(s, d):
        if len(STAGES[s]) == 1:
            a = STAGES[s][0]
            return {a: lax.rem(index[a] + d, sizes[a])}
        a, b = STAGES[s]
        place = lax.rem(index[a] * sizes[b] + index[b] + d, count(s))
        return {a: place // sizes[b], b: lax.rem(place, sizes[b])}

    peers = 0
    for s in range(len(STAGES)):
        for d in range(1, count(s)):
            pl.semaphore_signal(barrier, inc=1, device_id=peer(s, d), device_id_type=MESH)
            peers += 1

    have, toward = [], []
    for a in AXES:
        have += [index[a] > 0, index[a] < sizes[a] - 1]
        toward += [{a: lax.rem(index[a] + sizes[a] - 1, sizes[a])},
                   {a: lax.rem(index[a] + 1, sizes[a])}]
    half = [jnp.where(h, 0.5, 1.0).astype(F32) for h in have]

    def block(f):
        return slice(f * length, (f + 1) * length)

    exchanges = send.shape[0]
    for f in range(faces):
        @pl.when(jnp.logical_not(have[f]))
        def _():
            for e in range(exchanges):
                recv[e, f] = jnp.zeros((length, loads), BF16)

    def face_copy(e, f):
        return pltpu.make_async_remote_copy(
            src_ref=send.at[e, f], dst_ref=recv.at[e, f ^ 1], send_sem=send_sem.at[e, f],
            recv_sem=recv_sem.at[e, f ^ 1], device_id=toward[f], device_id_type=MESH)

    def face_arrival(e, f):
        return pltpu.make_async_remote_copy(
            src_ref=send.at[e, f], dst_ref=recv.at[e, f], send_sem=send_sem.at[e, f],
            recv_sem=recv_sem.at[e, f], device_id=toward[f], device_id_type=MESH)

    def post(e, f, value):
        send[e, f] = value.astype(BF16)

        @pl.when(have[f])
        def _():
            face_copy(e, f).start()

    def jumped(e, f):
        @pl.when(have[f])
        def _():
            face_arrival(e, f).wait_recv()
        return send[e, f].astype(F32) - recv[e, f].astype(F32)

    def apply(op, vector, take):
        x = vector[...]
        for g in range(0, faces, GROUP):
            y = dot(op[g * length:(g + GROUP) * length, :], x)
            for f in range(g, g + GROUP):
                take(f, y[block(f - g), :])

    def red_copy(k, s, d):
        return pltpu.make_async_remote_copy(
            src_ref=red_out.at[k, s], dst_ref=red_in.at[k, s, d - 1],
            send_sem=red_send_sem.at[k, s, d - 1], recv_sem=red_recv_sem.at[k, s, d - 1],
            device_id=peer(s, d), device_id_type=MESH)

    def red_start(k, s, value):
        red_out[k, s] = value
        for d in range(1, count(s)):
            red_copy(k, s, d).start()

    def red_finish(k, s):
        total = red_out[k, s]
        for d in range(1, count(s)):
            red_copy(k, s, d).wait_recv()
            total = total + red_in[k, s, d - 1]
        return total

    def pair(first, second):
        line = lax.broadcasted_iota(jnp.int32, (8, loads), 0)
        return jnp.where(line == 0, first, jnp.where(line == 1, second, 0.0))

    def total_of(value):
        return jnp.sum(value, axis=0, keepdims=True)

    for copy in lists_in:
        copy.wait()
    lanes = lax.broadcasted_iota(jnp.int32, (length, length), 1)
    lines = lax.broadcasted_iota(jnp.int32, (length, length), 0)
    for f in range(faces):
        row = jnp.broadcast_to(rows[0, 0, :, block(f)], (length, length))
        weight = jnp.broadcast_to(2.0 / mult[0, 0, :, block(f)].astype(F32), (length, length))
        row_t = row.astype(F32).T.astype(jnp.int32)
        weight_t = weight.T
        for c in range(width // length):
            table[block(c), block(f)] = jnp.where(row == lines + c * length, 1.0, 0.0).astype(BF16)
            hit = row_t == lanes + c * length
            picks[block(f), block(c)] = jnp.where(hit, 1.0, 0.0).astype(BF16)
            wpicks[block(f), block(c)] = jnp.where(hit, weight_t, 0.0).astype(BF16)

    pl.semaphore_wait(barrier, peers)
    loads_in[0].wait()
    apply(picks, disp, lambda f, y: post(0, f, y))

    def gather(left, op, scale, result):
        for i in range(faces // 2):
            part = slice(2 * i * length, 2 * (i + 1) * length)
            temp[:, part] = dot(op[...], table[:, part]).astype(BF16)
        for i in range(faces // 2):
            part = slice(2 * i * length, 2 * (i + 1) * length)
            value = dot(left[...], temp[:, part])
            if scale is not None:
                value = value * scale[:, part]
            result[:, part] = value.astype(BF16)

    weight_row = 2.0 / mult[0, 0].astype(F32)
    loads_in[1].wait()
    gather(wpicks, schur, weight_row, op_b)

    for f in ARRIVE:
        value = jumped(0, f)
        res[block(f), :] = value
        vec[block(f), :] = value.astype(BF16)
    apply(op_b, vec, lambda f, y: post(1, f, y))
    loads_in[2].wait()
    gather(picks, flex, None, op_a)
    rho = jnp.zeros((1, loads), F32)
    for f in ARRIVE:
        value = jumped(1, f)
        smo[block(f), :] = value
        vec[block(f), :] = value.astype(BF16)
        rho = rho + half[f] * total_of(res[block(f), :] * value)

    alpha = rho_old = None
    for k in range(ITERS):
        last = k + 1 == ITERS
        e = 2 + 2 * k
        parts = []

        def energy(f, y):
            if not last:
                post(e, f, y)
            parts.append(total_of(smo[block(f), :] * y))

        apply(op_a, vec, energy)
        red_start(k, 0, pair(rho, sum(parts)))
        if last:
            red_start(k, 1, red_finish(k, 0))
        else:
            for f in ARRIVE:
                value = jumped(e, f)
                img[block(f), :] = value
                vec[block(f), :] = value.astype(BF16)
            red_start(k, 1, red_finish(k, 0))
            apply(op_b, vec, lambda f, y: post(e + 1, f, y))
        sums = red_finish(k, 1)
        rho_now, curve = sums[0:1, :], sums[1:2, :]
        if k == 0:
            beta = None
            alpha = rho_now / curve
        else:
            beta = rho_now / rho_old
            alpha = rho_now / (curve - beta * rho_now / alpha)
        rho_old = rho_now
        rho = jnp.zeros((1, loads), F32)
        for f in ARRIVE:
            b = block(f)
            p = smo[b, :] if beta is None else smo[b, :] + beta * way[b, :]
            total = alpha * p if beta is None else out[b, :] + alpha * p
            out[b, :] = total
            if last:
                continue
            way[b, :] = p
            q = jumped(e + 1, f)
            s = img[b, :]
            if beta is not None:
                q = q + beta * across[b, :]
                s = s + beta * along[b, :]
            across[b, :] = q
            along[b, :] = s
            r = res[b, :] - alpha * s
            z = smo[b, :] - alpha * q
            res[b, :] = r
            smo[b, :] = z
            vec[b, :] = z.astype(BF16)
            rho = rho + half[f] * total_of(r * z)

    for f in range(faces):
        @pl.when(have[f])
        def _():
            for e in range(exchanges):
                face_copy(e, f).wait_send()
    for k in range(ITERS):
        for s in range(len(STAGES)):
            for d in range(1, count(s)):
                red_copy(k, s, d).wait_send()


def shards(sizes, displacement, flexibility, schur, face_rows, multiplicity):
    width = flexibility.shape[-1]
    loads = displacement.shape[-1]
    slots = face_rows.shape[-1]
    length = slots // 6
    exchanges = 2 * ITERS
    most = max(math.prod(sizes[a] for a in names) for names in STAGES)
    stages = len(STAGES)
    vmem = pl.BlockSpec(memory_space=pltpu.VMEM)
    state = pltpu.VMEM((slots, loads), F32)
    result = pl.pallas_call(
        functools.partial(kernel, sizes),
        out_shape=jax.ShapeDtypeStruct((1, 1, 1, slots, loads), F32),
        in_specs=[pl.BlockSpec(memory_space=pltpu.HBM)] * 5,
        out_specs=vmem,
        scratch_shapes=[
            pltpu.VMEM((width, loads), BF16),
            pltpu.VMEM((width, width), BF16),
            pltpu.VMEM((width, width), BF16),
            pltpu.VMEM((1, 1, 1, slots), jnp.int32),
            pltpu.VMEM((1, 1, 1, slots), jnp.int32),
            pltpu.VMEM((width, slots), BF16),
            pltpu.VMEM((slots, width), BF16),
            pltpu.VMEM((slots, width), BF16),
            pltpu.VMEM((width, slots), BF16),
            pltpu.VMEM((slots, slots), BF16),
            pltpu.VMEM((slots, slots), BF16),
            pltpu.VMEM((exchanges, 6, length, loads), BF16),
            pltpu.VMEM((exchanges, 6, length, loads), BF16),
            state, state, state, state, state, state,
            pltpu.VMEM((slots, loads), BF16),
            pltpu.VMEM((ITERS, stages, 8, loads), F32),
            pltpu.VMEM((ITERS, stages, most, 8, loads), F32),
            pltpu.SemaphoreType.DMA((5,)),
            pltpu.SemaphoreType.DMA((exchanges, 6)),
            pltpu.SemaphoreType.DMA((exchanges, 6)),
            pltpu.SemaphoreType.DMA((ITERS, stages, most)),
            pltpu.SemaphoreType.DMA((ITERS, stages, most)),
        ],
        compiler_params=pltpu.CompilerParams(
            collective_id=0, has_side_effects=True, vmem_limit_bytes=63 * 1024 * 1024),
    )(
        displacement, flexibility, schur,
        face_rows.reshape(1, 1, 1, slots), multiplicity.reshape(1, 1, 1, slots),
    )
    return result


def solution(mesh):
    whole = P(*AXES, None, None)
    lists = P(*AXES, None)
    return jax.shard_map(
        functools.partial(shards, {a: mesh.shape[a] for a in AXES}),
        mesh=mesh,
        in_specs=(whole, whole, whole, lists, lists),
        out_specs=whole,
        check_vma=False,
    )
```

```python
import functools
import math

import jax
import jax.numpy as jnp
from jax import lax
from jax.experimental import pallas as pl
from jax.experimental.pallas import tpu as pltpu
from jax.sharding import PartitionSpec as P

ITERS = 3
AXES = ("gx", "gy", "gz")
STAGES = (("gz",), ("gx", "gy"))
GROUPS = ((0, 1), (1, 2), (2, 4), (4, 6))
ARRIVE = (4, 5, 2, 3, 0, 1)
MESH = pl.DeviceIdType.MESH
F32 = jnp.float32
BF16 = jnp.bfloat16


def dot(a, b):
    return jnp.dot(a, b, preferred_element_type=F32)


def kernel(sizes, disp_in, flex_in, schur_in, rows_in, mult_in, out_ref, disp, flex, schur,
           rows, mult, table, picks, wpicks, temp,
           op_a, op_b, send, recv, res, smo, img, along, across, way, vec, red_out, red_in,
           load_sem, send_sem, recv_sem, red_send_sem, red_recv_sem):
    lists_in = [pltpu.make_async_copy(rows_in, rows, load_sem.at[3]),
                pltpu.make_async_copy(mult_in, mult, load_sem.at[4])]
    loads_in = [pltpu.make_async_copy(a.at[0, 0, 0], b, load_sem.at[i])
                for i, (a, b) in enumerate(((disp_in, disp), (schur_in, schur), (flex_in, flex)))]
    for copy in lists_in + loads_in:
        copy.start()
    width, loads = disp.shape
    slots = rows.shape[-1]
    faces = 6
    length = slots // faces
    out = out_ref.at[0, 0, 0]
    index = {a: lax.axis_index(a) for a in AXES}
    barrier = pltpu.get_barrier_semaphore()

    def count(s):
        return math.prod(sizes[a] for a in STAGES[s])

    def peer(s, d):
        if len(STAGES[s]) == 1:
            a = STAGES[s][0]
            return {a: lax.rem(index[a] + d, sizes[a])}
        a, b = STAGES[s]
        place = lax.rem(index[a] * sizes[b] + index[b] + d, count(s))
        return {a: place // sizes[b], b: lax.rem(place, sizes[b])}

    peers = 0
    for s in range(len(STAGES)):
        for d in range(1, count(s)):
            pl.semaphore_signal(barrier, inc=1, device_id=peer(s, d), device_id_type=MESH)
            peers += 1

    have, toward = [], []
    for a in AXES:
        have += [index[a] > 0, index[a] < sizes[a] - 1]
        toward += [{a: lax.rem(index[a] + sizes[a] - 1, sizes[a])},
                   {a: lax.rem(index[a] + 1, sizes[a])}]
    half = [jnp.where(h, 0.5, 1.0).astype(F32) for h in have]

    def block(f):
        return slice(f * length, (f + 1) * length)

    exchanges = send.shape[0]
    for f in range(faces):
        @pl.when(jnp.logical_not(have[f]))
        def _():
            for e in range(exchanges):
                recv[e, f] = jnp.zeros((length, loads), BF16)

    def face_copy(e, f):
        return pltpu.make_async_remote_copy(
            src_ref=send.at[e, f], dst_ref=recv.at[e, f ^ 1], send_sem=send_sem.at[e, f],
            recv_sem=recv_sem.at[e, f ^ 1], device_id=toward[f], device_id_type=MESH)

    def face_arrival(e, f):
        return pltpu.make_async_remote_copy(
            src_ref=send.at[e, f], dst_ref=recv.at[e, f], send_sem=send_sem.at[e, f],
            recv_sem=recv_sem.at[e, f], device_id=toward[f], device_id_type=MESH)

    def post(e, f, value):
        send[e, f] = value.astype(BF16)

        @pl.when(have[f])
        def _():
            face_copy(e, f).start()

    def jumped(e, f):
        @pl.when(have[f])
        def _():
            face_arrival(e, f).wait_recv()
        return send[e, f].astype(F32) - recv[e, f].astype(F32)

    def apply(op, vector, take):
        x = vector[...]
        for g, end in GROUPS:
            y = dot(op[g * length:end * length, :], x)
            for f in range(g, end):
                take(f, y[block(f - g), :])

    def red_copy(k, s, d):
        return pltpu.make_async_remote_copy(
            src_ref=red_out.at[k, s], dst_ref=red_in.at[k, s, d - 1],
            send_sem=red_send_sem.at[k, s, d - 1], recv_sem=red_recv_sem.at[k, s, d - 1],
            device_id=peer(s, d), device_id_type=MESH)

    def red_start(k, s, value):
        red_out[k, s] = value
        for d in range(1, count(s)):
            red_copy(k, s, d).start()

    def red_finish(k, s):
        total = red_out[k, s]
        for d in range(1, count(s)):
            red_copy(k, s, d).wait_recv()
            total = total + red_in[k, s, d - 1]
        return total

    def pair(first, second):
        line = lax.broadcasted_iota(jnp.int32, (8, loads), 0)
        return jnp.where(line == 0, first, jnp.where(line == 1, second, 0.0))

    def total_of(value):
        return jnp.sum(value, axis=0, keepdims=True)

    for copy in lists_in:
        copy.wait()
    lanes = lax.broadcasted_iota(jnp.int32, (length, length), 1)
    lines = lax.broadcasted_iota(jnp.int32, (length, length), 0)
    for f in range(faces):
        row = jnp.broadcast_to(rows[0, 0, :, block(f)], (length, length))
        weight = jnp.broadcast_to(2.0 / mult[0, 0, :, block(f)].astype(F32), (length, length))
        row_t = row.astype(F32).T.astype(jnp.int32)
        weight_t = weight.T
        for c in range(width // length):
            table[block(c), block(f)] = jnp.where(row == lines + c * length, 1.0, 0.0).astype(BF16)
            hit = row_t == lanes + c * length
            picks[block(f), block(c)] = jnp.where(hit, 1.0, 0.0).astype(BF16)
            wpicks[block(f), block(c)] = jnp.where(hit, weight_t, 0.0).astype(BF16)

    pl.semaphore_wait(barrier, peers)
    loads_in[0].wait()
    apply(picks, disp, lambda f, y: post(0, f, y))

    def gather(left, op, scale, result):
        for i in range(faces // 2):
            part = slice(2 * i * length, 2 * (i + 1) * length)
            temp[:, part] = dot(op[...], table[:, part]).astype(BF16)
        for i in range(faces // 2):
            part = slice(2 * i * length, 2 * (i + 1) * length)
            value = dot(left[...], temp[:, part])
            if scale is not None:
                value = value * scale[:, part]
            result[:, part] = value.astype(BF16)

    weight_row = 2.0 / mult[0, 0].astype(F32)
    loads_in[1].wait()
    gather(wpicks, schur, weight_row, op_b)

    for f in ARRIVE:
        value = jumped(0, f)
        res[block(f), :] = value
        vec[block(f), :] = value.astype(BF16)
    apply(op_b, vec, lambda f, y: post(1, f, y))
    loads_in[2].wait()
    gather(picks, flex, None, op_a)
    rho = jnp.zeros((1, loads), F32)
    for f in ARRIVE:
        value = jumped(1, f)
        smo[block(f), :] = value
        vec[block(f), :] = value.astype(BF16)
        rho = rho + half[f] * total_of(res[block(f), :] * value)

    alpha = rho_old = None
    for k in range(ITERS):
        last = k + 1 == ITERS
        e = 2 + 2 * k
        parts = []

        def energy(f, y):
            if not last:
                post(e, f, y)
            parts.append(total_of(smo[block(f), :] * y))

        apply(op_a, vec, energy)
        red_start(k, 0, pair(rho, sum(parts)))
        if last:
            red_start(k, 1, red_finish(k, 0))
        else:
            for f in ARRIVE:
                value = jumped(e, f)
                img[block(f), :] = value
                vec[block(f), :] = value.astype(BF16)
            red_start(k, 1, red_finish(k, 0))
            apply(op_b, vec, lambda f, y: post(e + 1, f, y))
        sums = red_finish(k, 1)
        rho_now, curve = sums[0:1, :], sums[1:2, :]
        if k == 0:
            beta = None
            alpha = rho_now / curve
        else:
            beta = rho_now / rho_old
            alpha = rho_now / (curve - beta * rho_now / alpha)
        rho_old = rho_now
        rho = jnp.zeros((1, loads), F32)
        for f in ARRIVE:
            b = block(f)
            p = smo[b, :] if beta is None else smo[b, :] + beta * way[b, :]
            total = alpha * p if beta is None else out[b, :] + alpha * p
            out[b, :] = total
            if last:
                continue
            way[b, :] = p
            q = jumped(e + 1, f)
            s = img[b, :]
            if beta is not None:
                q = q + beta * across[b, :]
                s = s + beta * along[b, :]
            across[b, :] = q
            along[b, :] = s
            r = res[b, :] - alpha * s
            z = smo[b, :] - alpha * q
            res[b, :] = r
            smo[b, :] = z
            vec[b, :] = z.astype(BF16)
            rho = rho + half[f] * total_of(r * z)

    for f in range(faces):
        @pl.when(have[f])
        def _():
            for e in range(exchanges):
                face_copy(e, f).wait_send()
    for k in range(ITERS):
        for s in range(len(STAGES)):
            for d in range(1, count(s)):
                red_copy(k, s, d).wait_send()


def shards(sizes, displacement, flexibility, schur, face_rows, multiplicity):
    width = flexibility.shape[-1]
    loads = displacement.shape[-1]
    slots = face_rows.shape[-1]
    length = slots // 6
    exchanges = 2 * ITERS
    most = max(math.prod(sizes[a] for a in names) for names in STAGES)
    stages = len(STAGES)
    vmem = pl.BlockSpec(memory_space=pltpu.VMEM)
    state = pltpu.VMEM((slots, loads), F32)
    result = pl.pallas_call(
        functools.partial(kernel, sizes),
        out_shape=jax.ShapeDtypeStruct((1, 1, 1, slots, loads), F32),
        in_specs=[pl.BlockSpec(memory_space=pltpu.HBM)] * 5,
        out_specs=vmem,
        scratch_shapes=[
            pltpu.VMEM((width, loads), BF16),
            pltpu.VMEM((width, width), BF16),
            pltpu.VMEM((width, width), BF16),
            pltpu.VMEM((1, 1, 1, slots), jnp.int32),
            pltpu.VMEM((1, 1, 1, slots), jnp.int32),
            pltpu.VMEM((width, slots), BF16),
            pltpu.VMEM((slots, width), BF16),
            pltpu.VMEM((slots, width), BF16),
            pltpu.VMEM((width, slots), BF16),
            pltpu.VMEM((slots, slots), BF16),
            pltpu.VMEM((slots, slots), BF16),
            pltpu.VMEM((exchanges, 6, length, loads), BF16),
            pltpu.VMEM((exchanges, 6, length, loads), BF16),
            state, state, state, state, state, state,
            pltpu.VMEM((slots, loads), BF16),
            pltpu.VMEM((ITERS, stages, 8, loads), F32),
            pltpu.VMEM((ITERS, stages, most, 8, loads), F32),
            pltpu.SemaphoreType.DMA((5,)),
            pltpu.SemaphoreType.DMA((exchanges, 6)),
            pltpu.SemaphoreType.DMA((exchanges, 6)),
            pltpu.SemaphoreType.DMA((ITERS, stages, most)),
            pltpu.SemaphoreType.DMA((ITERS, stages, most)),
        ],
        compiler_params=pltpu.CompilerParams(
            collective_id=0, has_side_effects=True, vmem_limit_bytes=63 * 1024 * 1024),
    )(
        displacement, flexibility, schur,
        face_rows.reshape(1, 1, 1, slots), multiplicity.reshape(1, 1, 1, slots),
    )
    return result


def solution(mesh):
    whole = P(*AXES, None, None)
    lists = P(*AXES, None)
    return jax.shard_map(
        functools.partial(shards, {a: mesh.shape[a] for a in AXES}),
        mesh=mesh,
        in_specs=(whole, whole, whole, lists, lists),
        out_specs=whole,
        check_vma=False,
    )
```
